32 devices in a mesh: groups: 2 (over y), row: 4 (over z), col: 2 (over x), chan: 2 (over core).
Axes of the slice: x: 2, y: 2, z: 4, core: 2. Of those that a mesh axis runs over, the one named last changes fastest.
Arguments:
- pair: bfloat16 [128, 64, 128], P(('groups', 'row'), 'col', 'chan'), parts along dimension 0, may hold values from -6 to 6
- token_mask: int32 [128], P('groups'), parts along dimension 0, may hold values 0 or 1
- w_proj: bfloat16 [2, 4, 128, 128], P(None, None, None, 'chan'), may hold values from -0.5 to 0.5
- w_gate: bfloat16 [2, 128, 128], replicated, may hold values from -0.5 to 0.5
- w_out: bfloat16 [2, 128, 128], replicated, may hold values from -0.5 to 0.5
- in_gain: float32 [2, 128], replicated, may hold values from 0.5 to 1.5
- in_bias: float32 [2, 128], replicated, may hold values from -3 to 3
- out_gain: float32 [2, 128], replicated, may hold values from 0.5 to 1.5
- out_bias: float32 [2, 128], replicated, may hold values from -3 to 3
Outputs:
- updated: bfloat16 [128, 64, 128], P(('groups', 'row'), 'col', 'chan'), parts along dimension 0
The draws below stay inside these ranges and needn't reach their ends.
There are 2 independent parts, one for each index of `groups`. The reference program is written for one: setup_inputs(seed, part) draws one part's arguments, and reference() takes and returns one part's arrays. A program takes and returns all parts, laid end to end along the dimension named above; an argument that names none is the same for every part. Nothing has to cross between parts.
Inputs may be any that keep to these rules, and one draw needn't show every extreme that they name: `token_mask`: 1 marks a real token, 0 a padded one.
All inputs are finite; a program needn't handle non-finite values.
Results may differ from the reference program's by a relative error of at most 0.009.
Values may be sent and summed in bfloat16 or wider, within the bound.
A program may use at most 64 MiB of HBM per device.

```python
import jax
import jax.numpy as jnp
from jax import lax

PAIR_CH = 128
HIDDEN_SIZE = 128
LENGTH = 64


def plant(entries, own_key, low, largest):
    longest = entries.shape.index(max(entries.shape))
    spots = []
    for shift in (0, 1):
        where = [jax.random.randint(jax.random.fold_in(own_key, axis), (), 0, length) for axis, length in enumerate(entries.shape)]
        where[longest] = (where[longest] + shift) % entries.shape[longest]
        spots.append(tuple(where))
    return entries.at[spots[0]].set(low).at[spots[1]].set(largest)


def block_scale(own_key, dims, split, smallest, largest):
    factor_of, own = 1.0, jax.random.fold_in(own_key, 6)
    for axis_at, parts in split:
        draws = jnp.exp(jax.random.uniform(jax.random.fold_in(own, axis_at), (parts,), jnp.float32, smallest / len(split), largest / len(split)))
        factor_of = factor_of * jnp.repeat(draws, dims[axis_at] // parts).reshape([-1 if axis == axis_at else 1 for axis in range(len(dims))])
    return factor_of


def scatter_about(rng, dims, deviation, bound, pieces=(), held_as=jnp.bfloat16):
    entries = deviation * jax.random.normal(rng, dims, jnp.float32)
    if pieces:
        entries = entries * block_scale(rng, dims, pieces, -0.22, 0.18)
    return jnp.clip(entries, -bound, bound).astype(held_as)


def setup_inputs(seed: int = 0, part: int = 0) -> dict:
    seeds = jax.random.split(jax.random.key(seed), 10)
    part_keys = jax.random.split(jax.random.fold_in(seeds[9], part), 10)
    pair = scatter_about(part_keys[0], (LENGTH, LENGTH, PAIR_CH), 1.0, 6.0, ((0, 4), (1, 2), (2, 2)))
    token_mask = plant((jax.random.randint(part_keys[1], (LENGTH,), 0, 8) < 7).astype(jnp.int32), jax.random.fold_in(part_keys[1], 1), 0, 1)
    w_proj = scatter_about(seeds[2], (2, 4, PAIR_CH, HIDDEN_SIZE), PAIR_CH ** -0.5, 0.5, ((3, 2),))
    w_gate = scatter_about(seeds[3], (2, PAIR_CH, PAIR_CH), PAIR_CH ** -0.5, 0.5)
    w_out = scatter_about(seeds[4], (2, HIDDEN_SIZE, PAIR_CH), HIDDEN_SIZE ** -0.5, 0.5)
    in_gain = jnp.clip(1.0 + 0.1 * jax.random.normal(seeds[5], (2, PAIR_CH), jnp.float32), 0.5, 1.5)
    in_bias = scatter_about(seeds[6], (2, PAIR_CH), 0.5, 3.0, (), jnp.float32)
    out_gain = jnp.clip(1.0 + 0.1 * jax.random.normal(seeds[7], (2, HIDDEN_SIZE), jnp.float32), 0.5, 1.5)
    out_bias = scatter_about(seeds[8], (2, HIDDEN_SIZE), 0.5, 3.0, (), jnp.float32)
    return dict(pair=pair, token_mask=token_mask, w_proj=w_proj, w_gate=w_gate, w_out=w_out, in_gain=in_gain, in_bias=in_bias, out_gain=out_gain, out_bias=out_bias)


epsilon = 1e-05

def normalize(values, gain, bias):
    center = lax.optimization_barrier(jnp.mean(values, axis=-1, keepdims=True))
    spread = lax.optimization_barrier(jnp.mean(jnp.square(values - center), axis=-1, keepdims=True))
    return (values - center) * lax.rsqrt(spread + epsilon) * gain + bias

def triangle(pair, token_mask, direction, w_proj, w_gate, w_out, in_gain, in_bias, out_gain, out_bias):
    values = pair.astype(jnp.float32)
    normed = normalize(values, in_gain[direction], in_bias[direction]).astype(jnp.bfloat16)
    normed_wide = normed.astype(jnp.float32)
    weights = w_proj[direction].astype(jnp.float32)
    masked = token_mask.astype(jnp.float32)
    pair_mask = (masked[:, None] * masked[None, :])[:, :, None]
    left_value = jnp.einsum('ijc,ch->ijh', normed_wide, weights[0])
    left_gate = jnp.einsum('ijc,ch->ijh', normed_wide, weights[1])
    left = (jax.nn.sigmoid(left_gate) * left_value * pair_mask).astype(jnp.bfloat16)
    right_value = jnp.einsum('ijc,ch->ijh', normed_wide, weights[2])
    right_gate = jnp.einsum('ijc,ch->ijh', normed_wide, weights[3])
    right = (jax.nn.sigmoid(right_gate) * right_value * pair_mask).astype(jnp.bfloat16)
    if direction == 0:
        mixed = jnp.einsum('ikh,jkh->ijh', left.astype(jnp.float32), right.astype(jnp.float32))
    else:
        mixed = jnp.einsum('kih,kjh->ijh', left.astype(jnp.float32), right.astype(jnp.float32))
    mixed = mixed.astype(jnp.bfloat16)
    mixed_norm = normalize(mixed.astype(jnp.float32), out_gain[direction], out_bias[direction]).astype(jnp.bfloat16)
    gate = jax.nn.sigmoid(jnp.einsum('ijc,ce->ije', normed_wide, w_gate[direction].astype(jnp.float32)))
    update = gate * jnp.einsum('ijh,hc->ijc', mixed_norm.astype(jnp.float32), w_out[direction].astype(jnp.float32))
    return (values + update).astype(jnp.bfloat16)

def reference(pair, token_mask, w_proj, w_gate, w_out, in_gain, in_bias, out_gain, out_bias):
    first = triangle(pair, token_mask, 0, w_proj, w_gate, w_out, in_gain, in_bias, out_gain, out_bias)
    return triangle(first, token_mask, 1, w_proj, w_gate, w_out, in_gain, in_bias, out_gain, out_bias)
```

```python
import functools

import jax
import jax.numpy as jnp
from jax import lax
from jax.experimental import pallas as pl
from jax.experimental.pallas import tpu as pltpu
from jax.sharding import PartitionSpec as P

epsilon = 1e-05
MESH = pl.DeviceIdType.MESH


def normalize(values, gain, bias):
    center = jnp.mean(values, axis=-1, keepdims=True)
    off = values - center
    spread = jnp.mean(off * off, axis=-1, keepdims=True)
    return off * lax.rsqrt(spread + epsilon) * gain + bias


def sigmoid(values):
    return 0.5 * jnp.tanh(0.5 * values) + 0.5


def kernel(
    rows, cols, chans, edge,
    pair_ref, mask_ref, w_proj_ref, w_gate_ref, w_out_ref,
    in_gain_ref, in_bias_ref, out_gain_ref, out_bias_ref, out_ref,
    raw, mid, fin, w_half, w_full, mask_col, spread_op, tile_op, values, normed_own,
    send_sems, raw_sems, mid_sems, w_sems, fin_sems,
):
    group = lax.axis_index("groups")
    r, c, h = lax.axis_index("row"), lax.axis_index("col"), lax.axis_index("chan")
    blocks = rows
    area = edge * edge
    length = edge * blocks
    half = pair_ref.shape[2]
    q = c * chans + h
    away = jnp.where(q == r, 0, 1)
    off_diagonal = q != r
    sibling = (group, r, c, 1 - h)

    def plane(step):
        other = lax.rem(q + step, blocks)
        return (group, r, other // chans, lax.rem(other, chans))

    def column(step):
        return (group, lax.rem(r + step, rows), r // chans, lax.rem(r, chans))

    barrier = pltpu.get_barrier_semaphore()
    for step in range(1, blocks):
        pl.semaphore_signal(barrier, inc=1, device_id=plane(step), device_id_type=MESH)

    @pl.when(off_diagonal)
    def _():
        for other in range(blocks):
            pl.semaphore_signal(
                barrier, inc=1,
                device_id=(group, q, other // chans, other % chans), device_id_type=MESH,
            )

    own = pair_ref[...].astype(jnp.float32)
    packed = jnp.concatenate([own[:, :edge, :], own[:, edge:, :]], axis=-1)
    raw[0, q] = packed.reshape(area, 2 * half).astype(jnp.bfloat16)
    pl.semaphore_wait(barrier, 2 * (blocks - 1))

    def send_block(buffer, sems, base):
        copies = []
        for step in range(1, blocks):
            copies.append(pltpu.make_async_remote_copy(
                src_ref=buffer.at[0, q], dst_ref=buffer.at[1, q],
                send_sem=send_sems.at[base + step], recv_sem=sems.at[1, q],
                device_id=column(step), device_id_type=MESH,
            ))
        for step in range(1, blocks):
            copies.append(pltpu.make_async_remote_copy(
                src_ref=buffer.at[0, q], dst_ref=buffer.at[0, q],
                send_sem=send_sems.at[base + blocks + step], recv_sem=sems.at[0, q],
                device_id=plane(step), device_id_type=MESH,
            ))
        for copy in copies:
            copy.start()
        return copies

    def wait_block(buffer, sems, which, slot):
        pltpu.make_async_remote_copy(
            src_ref=buffer.at[0, q], dst_ref=buffer.at[which, slot],
            send_sem=send_sems.at[0], recv_sem=sems.at[which, slot],
            device_id=sibling, device_id_type=MESH,
        ).wait_recv()

    def wait_plane(buffer, sems, slot):
        @pl.when(slot != q)
        def _():
            wait_block(buffer, sems, 0, slot)

    def wait_column(buffer, sems, slot):
        @pl.when(off_diagonal)
        def _():
            wait_block(buffer, sems, 1, slot)

    started = send_block(raw, raw_sems, 0)
    w_copy = pltpu.make_async_remote_copy(
        src_ref=w_proj_ref, dst_ref=w_half, send_sem=w_sems.at[0], recv_sem=w_sems.at[1],
        device_id=sibling, device_id_type=MESH,
    )
    w_copy.start()

    ids = lax.broadcasted_iota(jnp.int32, (length, length), 0)
    lanes = lax.broadcasted_iota(jnp.int32, (length, length), 1)
    flags = jnp.where(ids == lanes, mask_ref[...].astype(jnp.float32), 0.0)
    mask_col[...] = jnp.broadcast_to(jnp.sum(flags, axis=-1, keepdims=True), (length, 2 * half))

    w_copy.wait()
    first_chan = h == 0
    for u in range(2):
        for w in range(4):
            mine = w_proj_ref[u, w].astype(jnp.float32)
            theirs = w_half[u, w].astype(jnp.float32)
            low = jnp.where(first_chan, mine, theirs)
            high = jnp.where(first_chan, theirs, mine)
            full = jnp.concatenate([low, high], axis=-1).astype(jnp.bfloat16)
            w_full[u, w // 2, :, (w % 2) * 2 * half:(w % 2 + 1) * 2 * half] = full

    lower = lax.broadcasted_iota(jnp.int32, (area, 2 * half), 1) < half

    def unpacked(which, pair_slot):
        even = raw[which, chans * pair_slot].astype(jnp.float32)
        odd = raw[which, chans * pair_slot + 1].astype(jnp.float32)
        first = jnp.where(lower, even, pltpu.roll(odd, half, 1))
        second = jnp.where(lower, pltpu.roll(even, half, 1), odd)
        return first, second

    def project(u, side, wide, outer_block, inner_block, keep):
        normed = normalize(
            wide, in_gain_ref[u:u + 1, :], in_bias_ref[u:u + 1, :]
        ).astype(jnp.bfloat16)
        if keep is not None:
            values[keep] = wide.astype(jnp.bfloat16)
            normed_own[keep] = normed
        both = jnp.dot(normed, w_full[u, side], preferred_element_type=jnp.float32)
        outer = mask_col[pl.ds(outer_block * edge, edge), :]
        inner = mask_col[pl.ds(inner_block * edge, edge), :]
        mask = outer[:, None, :] * inner[None, :, :]
        gated = sigmoid(both[:, 2 * half:]) * both[:, :2 * half]
        gated = gated.reshape(edge, edge, 2 * half) * mask
        return gated.astype(jnp.bfloat16).astype(jnp.float32)

    def mix(row_of):
        def step(k, totals):
            tile = tile_op[pl.ds(k * edge, edge), :]
            return tuple(
                totals[i] + spread_op[pl.ds(row_of(i, k), 1), :] * tile for i in range(edge)
            )
        zero = tuple(jnp.zeros((edge, 2 * half), jnp.float32) for _ in range(edge))
        totals = lax.fori_loop(0, length, step, zero, unroll=4)
        return jnp.concatenate(totals, axis=0)

    def finish(u, mixed, block):
        mixed = mixed.astype(jnp.bfloat16).astype(jnp.float32)
        mixed_norm = normalize(
            mixed, out_gain_ref[u:u + 1, :], out_bias_ref[u:u + 1, :]
        ).astype(jnp.bfloat16)
        projected = jnp.dot(mixed_norm, w_out_ref[u], preferred_element_type=jnp.float32)
        gate = sigmoid(jnp.dot(normed_own[block], w_gate_ref[u], preferred_element_type=jnp.float32))
        return (values[block].astype(jnp.float32) + gate * projected).astype(jnp.bfloat16)

    def right_blocks(pair_slot, carry):
        for part in range(chans):
            wait_plane(raw, raw_sems, chans * pair_slot + part)
        for part, wide in enumerate(unpacked(0, pair_slot)):
            inner = chans * pair_slot + part
            gated = project(0, 1, wide, r, inner, None)
            for j in range(edge):
                tile_op[pl.ds(inner * area + j, edge, stride=edge), :] = gated[j]
        return carry

    lax.fori_loop(0, cols, right_blocks, 0)

    def left_blocks(pair_slot, carry):
        for part in range(chans):
            wait_column(raw, raw_sems, chans * pair_slot + part)
        for part, wide in enumerate(unpacked(away, pair_slot)):
            inner = chans * pair_slot + part
            gated = project(0, 0, wide, q, inner, inner)
            for i in range(edge):
                spread_op[pl.ds(i * length + inner * edge, edge), :] = gated[i]
        return carry

    lax.fori_loop(0, cols, left_blocks, 0)
    mid[0, q] = finish(0, mix(lambda i, k: i * length + k), r)

    started += send_block(mid, mid_sems, 2 * blocks)

    def left_columns(slot, carry):
        wait_plane(mid, mid_sems, slot)
        gated = project(1, 0, mid[0, slot].astype(jnp.float32), slot, r, None)
        spread_op[pl.ds(slot * area, area), :] = gated.reshape(area, 2 * half)
        return carry

    lax.fori_loop(0, blocks, left_columns, 0)

    def right_columns(slot, carry):
        wait_column(mid, mid_sems, slot)
        gated = project(1, 1, mid[away, slot].astype(jnp.float32), slot, q, slot)
        tile_op[pl.ds(slot * area, area), :] = gated.reshape(area, 2 * half)
        return carry

    lax.fori_loop(0, blocks, right_columns, 0)
    fin[h] = finish(1, mix(lambda i, k: k * edge + i), r)

    last = pltpu.make_async_remote_copy(
        src_ref=fin.at[h], dst_ref=fin.at[h], send_sem=fin_sems.at[0], recv_sem=fin_sems.at[1],
        device_id=sibling, device_id_type=MESH,
    )
    last.start()
    for copy in started:
        copy.wait_send()
    last.wait()
    for part in range(chans):
        block = fin[part].astype(jnp.float32)
        piece = jnp.where(first_chan, block[:, :half], block[:, half:])
        out_ref[:, part * edge:(part + 1) * edge, :] = (
            piece.reshape(edge, edge, half).astype(jnp.bfloat16)
        )


def local(sizes, pair, token_mask, w_proj, w_gate, w_out, in_gain, in_bias, out_gain, out_bias):
    rows, cols, chans = sizes
    edge, wide_cols, half = pair.shape
    blocks, area, length = rows, edge * edge, token_mask.shape[0]
    full = chans * half
    assert chans == 2 and rows == cols * chans and wide_cols == chans * edge
    vmem = pl.BlockSpec(memory_space=pltpu.VMEM)
    return pl.pallas_call(
        functools.partial(kernel, rows, cols, chans, edge),
        out_shape=jax.ShapeDtypeStruct(pair.shape, pair.dtype),
        in_specs=[vmem] * 9,
        out_specs=vmem,
        scratch_shapes=[
            pltpu.VMEM((2, blocks, area, full), jnp.bfloat16),
            pltpu.VMEM((2, blocks, area, full), jnp.bfloat16),
            pltpu.VMEM((chans, area, full), jnp.bfloat16),
            pltpu.VMEM(w_proj.shape, jnp.bfloat16),
            pltpu.VMEM((2, 2, full, 2 * full), jnp.bfloat16),
            pltpu.VMEM((length, full), jnp.float32),
            pltpu.VMEM((edge * length, full), jnp.float32),
            pltpu.VMEM((edge * length, full), jnp.float32),
            pltpu.VMEM((blocks, area, full), jnp.bfloat16),
            pltpu.VMEM((blocks, area, full), jnp.bfloat16),
            pltpu.SemaphoreType.DMA((4 * blocks,)),
            pltpu.SemaphoreType.DMA((2, blocks)),
            pltpu.SemaphoreType.DMA((2, blocks)),
            pltpu.SemaphoreType.DMA((2,)),
            pltpu.SemaphoreType.DMA((2,)),
        ],
        compiler_params=pltpu.CompilerParams(
            collective_id=0, has_side_effects=True, vmem_limit_bytes=48 * 1024 * 1024
        ),
    )(pair, token_mask.reshape(1, length), w_proj, w_gate, w_out, in_gain, in_bias, out_gain, out_bias)


def solution(mesh):
    sizes = tuple(mesh.shape[name] for name in ("row", "col", "chan"))
    return jax.shard_map(
        functools.partial(local, sizes),
        mesh=mesh,
        in_specs=(
            P(("groups", "row"), "col", "chan"),
            P("groups"),
            P(None, None, None, "chan"),
            P(),
            P(),
            P(),
            P(),
            P(),
            P(),
        ),
        out_specs=P(("groups", "row"), "col", "chan"),
        check_vma=False,
    )
```

```python
import functools

import jax
import jax.numpy as jnp
from jax import lax
from jax.experimental import pallas as pl
from jax.experimental.pallas import tpu as pltpu
from jax.sharding import PartitionSpec as P

epsilon = 1e-05
MESH = pl.DeviceIdType.MESH


def normalize(values, gain, bias):
    center = jnp.mean(values, axis=-1, keepdims=True)
    off = values - center
    spread = jnp.mean(off * off, axis=-1, keepdims=True)
    return off * lax.rsqrt(spread + epsilon) * gain + bias


def sigmoid(values):
    return 0.5 * jnp.tanh(0.5 * values) + 0.5


def kernel(
    rows, cols, chans, edge,
    pair_ref, mask_ref, w_proj_ref, w_gate_ref, w_out_ref,
    in_gain_ref, in_bias_ref, out_gain_ref, out_bias_ref, out_ref,
    raw, mid, fin, w_half, w_full, mask_col, spread_op, tile_op, values, normed_own,
    send_sems, raw_sems, mid_sems, w_sems, fin_sems,
):
    group = lax.axis_index("groups")
    r, c, h = lax.axis_index("row"), lax.axis_index("col"), lax.axis_index("chan")
    blocks = rows
    area = edge * edge
    length = edge * blocks
    half = pair_ref.shape[2]
    q = c * chans + h
    away = jnp.where(q == r, 0, 1)
    off_diagonal = q != r
    sibling = (group, r, c, 1 - h)

    def plane(step):
        other = lax.rem(q + step, blocks)
        return (group, r, other // chans, lax.rem(other, chans))

    def column(step):
        return (group, lax.rem(r + step, rows), r // chans, lax.rem(r, chans))

    barrier = pltpu.get_barrier_semaphore()
    for step in range(1, blocks):
        pl.semaphore_signal(barrier, inc=1, device_id=plane(step), device_id_type=MESH)

    @pl.when(off_diagonal)
    def _():
        for other in range(blocks):
            pl.semaphore_signal(
                barrier, inc=1,
                device_id=(group, q, other // chans, other % chans), device_id_type=MESH,
            )

    own = pair_ref[...].astype(jnp.float32)
    packed = jnp.concatenate([own[:, :edge, :], own[:, edge:, :]], axis=-1)
    raw[0, q] = packed.reshape(area, 2 * half).astype(jnp.bfloat16)
    pl.semaphore_wait(barrier, 2 * (blocks - 1))

    def send_block(buffer, sems, base):
        copies = []
        for step in range(1, blocks):
            copies.append(pltpu.make_async_remote_copy(
                src_ref=buffer.at[0, q], dst_ref=buffer.at[1, q],
                send_sem=send_sems.at[base + step], recv_sem=sems.at[1, q],
                device_id=column(step), device_id_type=MESH,
            ))
        for step in range(cols):
            target = (group, r, lax.rem(c + step, cols), h) if step else sibling
            copies.append(pltpu.make_async_remote_copy(
                src_ref=buffer.at[0, q], dst_ref=buffer.at[0, q],
                send_sem=send_sems.at[base + blocks + step], recv_sem=sems.at[0, q],
                device_id=target, device_id_type=MESH,
            ))
        for copy in copies:
            copy.start()
        return copies

    def wait_block(buffer, sems, which, slot):
        pltpu.make_async_remote_copy(
            src_ref=buffer.at[0, q], dst_ref=buffer.at[which, slot],
            send_sem=send_sems.at[0], recv_sem=sems.at[which, slot],
            device_id=sibling, device_id_type=MESH,
        ).wait_recv()

    def hand_on(buffer, sems, base):
        copies = []
        for step in range(1, cols):
            slot = lax.rem(c + step, cols) * chans + h
            wait_block(buffer, sems, 0, slot)
            copy = pltpu.make_async_remote_copy(
                src_ref=buffer.at[0, slot], dst_ref=buffer.at[0, slot],
                send_sem=send_sems.at[base + blocks + cols - 1 + step],
                recv_sem=sems.at[0, slot],
                device_id=sibling, device_id_type=MESH,
            )
            copy.start()
            copies.append(copy)
        return copies

    def wait_column(buffer, sems, slot):
        @pl.when(off_diagonal)
        def _():
            wait_block(buffer, sems, 1, slot)

    started = send_block(raw, raw_sems, 0)
    w_copy = pltpu.make_async_remote_copy(
        src_ref=w_proj_ref, dst_ref=w_half, send_sem=w_sems.at[0], recv_sem=w_sems.at[1],
        device_id=sibling, device_id_type=MESH,
    )
    w_copy.start()

    ids = lax.broadcasted_iota(jnp.int32, (length, length), 0)
    lanes = lax.broadcasted_iota(jnp.int32, (length, length), 1)
    flags = jnp.where(ids == lanes, mask_ref[...].astype(jnp.float32), 0.0)
    mask_col[...] = jnp.broadcast_to(jnp.sum(flags, axis=-1, keepdims=True), (length, 2 * half))

    w_copy.wait()
    first_chan = h == 0
    for u in range(2):
        for w in range(4):
            mine = w_proj_ref[u, w].astype(jnp.float32)
            theirs = w_half[u, w].astype(jnp.float32)
            low = jnp.where(first_chan, mine, theirs)
            high = jnp.where(first_chan, theirs, mine)
            full = jnp.concatenate([low, high], axis=-1).astype(jnp.bfloat16)
            w_full[u, w // 2, :, (w % 2) * 2 * half:(w % 2 + 1) * 2 * half] = full

    lower = lax.broadcasted_iota(jnp.int32, (area, 2 * half), 1) < half

    def unpacked(which, pair_slot):
        even = raw[which, chans * pair_slot].astype(jnp.float32)
        odd = raw[which, chans * pair_slot + 1].astype(jnp.float32)
        first = jnp.where(lower, even, pltpu.roll(odd, half, 1))
        second = jnp.where(lower, pltpu.roll(even, half, 1), odd)
        return first, second

    def project(u, side, wide, outer_block, inner_block, keep):
        normed = normalize(
            wide, in_gain_ref[u:u + 1, :], in_bias_ref[u:u + 1, :]
        ).astype(jnp.bfloat16)
        if keep is not None:
            values[keep] = wide.astype(jnp.bfloat16)
            normed_own[keep] = normed
        both = jnp.dot(normed, w_full[u, side], preferred_element_type=jnp.float32)
        outer = mask_col[pl.ds(outer_block * edge, edge), :]
        inner = mask_col[pl.ds(inner_block * edge, edge), :]
        mask = outer[:, None, :] * inner[None, :, :]
        gated = sigmoid(both[:, 2 * half:]) * both[:, :2 * half]
        gated = gated.reshape(edge, edge, 2 * half) * mask
        return gated.astype(jnp.bfloat16).astype(jnp.float32)

    def mix(row_of):
        def step(k, totals):
            tile = tile_op[pl.ds(k * edge, edge), :]
            return tuple(
                totals[i] + spread_op[pl.ds(row_of(i, k), 1), :] * tile for i in range(edge)
            )
        zero = tuple(jnp.zeros((edge, 2 * half), jnp.float32) for _ in range(edge))
        totals = lax.fori_loop(0, length, step, zero, unroll=4)
        return jnp.concatenate(totals, axis=0)

    def finish(u, mixed, block):
        mixed = mixed.astype(jnp.bfloat16).astype(jnp.float32)
        mixed_norm = normalize(
            mixed, out_gain_ref[u:u + 1, :], out_bias_ref[u:u + 1, :]
        ).astype(jnp.bfloat16)
        projected = jnp.dot(mixed_norm, w_out_ref[u], preferred_element_type=jnp.float32)
        gate = sigmoid(jnp.dot(normed_own[block], w_gate_ref[u], preferred_element_type=jnp.float32))
        return (values[block].astype(jnp.float32) + gate * projected).astype(jnp.bfloat16)

    def right_blocks(step, carry):
        pair_slot = lax.rem(c + step, cols)
        wait_block(raw, raw_sems, 0, chans * pair_slot + 1 - h)
        for part, wide in enumerate(unpacked(0, pair_slot)):
            inner = chans * pair_slot + part
            gated = project(0, 1, wide, r, inner, None)
            for j in range(edge):
                tile_op[pl.ds(inner * area + j, edge, stride=edge), :] = gated[j]
        return carry

    right_blocks(0, 0)
    started += hand_on(raw, raw_sems, 0)
    lax.fori_loop(1, cols, right_blocks, 0)

    def left_blocks(pair_slot, carry):
        for part in range(chans):
            wait_column(raw, raw_sems, chans * pair_slot + part)
        for part, wide in enumerate(unpacked(away, pair_slot)):
            inner = chans * pair_slot + part
            gated = project(0, 0, wide, q, inner, inner)
            for i in range(edge):
                spread_op[pl.ds(i * length + inner * edge, edge), :] = gated[i]
        return carry

    lax.fori_loop(0, cols, left_blocks, 0)
    mid[0, q] = finish(0, mix(lambda i, k: i * length + k), r)

    started += send_block(mid, mid_sems, 2 * blocks)

    def left_columns(step, carry):
        pair_slot = lax.rem(c + step, cols)
        wait_block(mid, mid_sems, 0, chans * pair_slot + 1 - h)
        for part in range(chans):
            slot = chans * pair_slot + part
            gated = project(1, 0, mid[0, slot].astype(jnp.float32), slot, r, None)
            spread_op[pl.ds(slot * area, area), :] = gated.reshape(area, 2 * half)
        return carry

    left_columns(0, 0)
    started += hand_on(mid, mid_sems, 2 * blocks)
    lax.fori_loop(1, cols, left_columns, 0)

    def right_columns(slot, carry):
        wait_column(mid, mid_sems, slot)
        gated = project(1, 1, mid[away, slot].astype(jnp.float32), slot, q, slot)
        tile_op[pl.ds(slot * area, area), :] = gated.reshape(area, 2 * half)
        return carry

    lax.fori_loop(0, blocks, right_columns, 0)
    fin[h] = finish(1, mix(lambda i, k: k * edge + i), r)

    last = pltpu.make_async_remote_copy(
        src_ref=fin.at[h], dst_ref=fin.at[h], send_sem=fin_sems.at[0], recv_sem=fin_sems.at[1],
        device_id=sibling, device_id_type=MESH,
    )
    last.start()
    for copy in started:
        copy.wait_send()
    last.wait()
    for part in range(chans):
        block = fin[part].astype(jnp.float32)
        piece = jnp.where(first_chan, block[:, :half], block[:, half:])
        out_ref[:, part * edge:(part + 1) * edge, :] = (
            piece.reshape(edge, edge, half).astype(jnp.bfloat16)
        )


def local(sizes, pair, token_mask, w_proj, w_gate, w_out, in_gain, in_bias, out_gain, out_bias):
    rows, cols, chans = sizes
    edge, wide_cols, half = pair.shape
    blocks, area, length = rows, edge * edge, token_mask.shape[0]
    full = chans * half
    assert chans == 2 and rows == cols * chans and wide_cols == chans * edge
    vmem = pl.BlockSpec(memory_space=pltpu.VMEM)
    return pl.pallas_call(
        functools.partial(kernel, rows, cols, chans, edge),
        out_shape=jax.ShapeDtypeStruct(pair.shape, pair.dtype),
        in_specs=[vmem] * 9,
        out_specs=vmem,
        scratch_shapes=[
            pltpu.VMEM((2, blocks, area, full), jnp.bfloat16),
            pltpu.VMEM((2, blocks, area, full), jnp.bfloat16),
            pltpu.VMEM((chans, area, full), jnp.bfloat16),
            pltpu.VMEM(w_proj.shape, jnp.bfloat16),
            pltpu.VMEM((2, 2, full, 2 * full), jnp.bfloat16),
            pltpu.VMEM((length, full), jnp.float32),
            pltpu.VMEM((edge * length, full), jnp.float32),
            pltpu.VMEM((edge * length, full), jnp.float32),
            pltpu.VMEM((blocks, area, full), jnp.bfloat16),
            pltpu.VMEM((blocks, area, full), jnp.bfloat16),
            pltpu.SemaphoreType.DMA((4 * blocks,)),
            pltpu.SemaphoreType.DMA((2, blocks)),
            pltpu.SemaphoreType.DMA((2, blocks)),
            pltpu.SemaphoreType.DMA((2,)),
            pltpu.SemaphoreType.DMA((2,)),
        ],
        compiler_params=pltpu.CompilerParams(
            collective_id=0, has_side_effects=True, vmem_limit_bytes=48 * 1024 * 1024
        ),
    )(pair, token_mask.reshape(1, length), w_proj, w_gate, w_out, in_gain, in_bias, out_gain, out_bias)


def solution(mesh):
    sizes = tuple(mesh.shape[name] for name in ("row", "col", "chan"))
    return jax.shard_map(
        functools.partial(local, sizes),
        mesh=mesh,
        in_specs=(
            P(("groups", "row"), "col", "chan"),
            P("groups"),
            P(None, None, None, "chan"),
            P(),
            P(),
            P(),
            P(),
            P(),
            P(),
        ),
        out_specs=P(("groups", "row"), "col", "chan"),
        check_vma=False,
    )
```

```python
import functools

import jax
import jax.numpy as jnp
from jax import lax
from jax.experimental import pallas as pl
from jax.experimental.pallas import tpu as pltpu
from jax.sharding import PartitionSpec as P

epsilon = 1e-05
MESH = pl.DeviceIdType.MESH


def normalize(values, gain, bias):
    center = jnp.mean(values, axis=-1, keepdims=True)
    off = values - center
    spread = jnp.mean(off * off, axis=-1, keepdims=True)
    return off * lax.rsqrt(spread + epsilon) * gain + bias


def sigmoid(values):
    return 0.5 * jnp.tanh(0.5 * values) + 0.5


def kernel(
    rows, cols, chans, edge,
    pair_ref, mask_ref, w_proj_ref, w_gate_ref, w_out_ref,
    in_gain_ref, in_bias_ref, out_gain_ref, out_bias_ref, out_ref,
    raw, mid, fin, w_half, w_full, mask_col, spread_op, tile_op, values, normed_own,
    send_sems, raw_sems, mid_sems, w_sems, fin_sems,
):
    group = lax.axis_index("groups")
    r, c, h = lax.axis_index("row"), lax.axis_index("col"), lax.axis_index("chan")
    blocks = rows
    area = edge * edge
    length = edge * blocks
    half = pair_ref.shape[2]
    q = c * chans + h
    away = jnp.where(q == r, 0, 1)
    off_diagonal = q != r
    sibling = (group, r, c, 1 - h)

    def plane(step):
        other = lax.rem(q + step, blocks)
        return (group, r, other // chans, lax.rem(other, chans))

    def column(step):
        return (group, lax.rem(r + step, rows), r // chans, lax.rem(r, chans))

    barrier = pltpu.get_barrier_semaphore()
    for step in range(1, blocks):
        pl.semaphore_signal(barrier, inc=1, device_id=plane(step), device_id_type=MESH)

    @pl.when(off_diagonal)
    def _():
        for other in range(blocks):
            pl.semaphore_signal(
                barrier, inc=1,
                device_id=(group, q, other // chans, other % chans), device_id_type=MESH,
            )

    own = pair_ref[...].astype(jnp.float32)
    packed = jnp.concatenate([own[:, :edge, :], own[:, edge:, :]], axis=-1)
    raw[0, q] = packed.reshape(area, 2 * half).astype(jnp.bfloat16)
    pl.semaphore_wait(barrier, 2 * (blocks - 1))

    def send_block(buffer, sems, base):
        copies = []
        for step in range(cols):
            target = (group, r, lax.rem(c + step, cols), h) if step else sibling
            copies.append(pltpu.make_async_remote_copy(
                src_ref=buffer.at[0, q], dst_ref=buffer.at[0, q],
                send_sem=send_sems.at[base + blocks + step], recv_sem=sems.at[0, q],
                device_id=target, device_id_type=MESH,
            ))
        for step in range(1, blocks):
            copies.append(pltpu.make_async_remote_copy(
                src_ref=buffer.at[0, q], dst_ref=buffer.at[1, q],
                send_sem=send_sems.at[base + step], recv_sem=sems.at[1, q],
                device_id=column(step), device_id_type=MESH,
            ))
        for copy in copies:
            copy.start()
        return copies

    def wait_block(buffer, sems, which, slot):
        pltpu.make_async_remote_copy(
            src_ref=buffer.at[0, q], dst_ref=buffer.at[which, slot],
            send_sem=send_sems.at[0], recv_sem=sems.at[which, slot],
            device_id=sibling, device_id_type=MESH,
        ).wait_recv()

    def hand_on(buffer, sems, base):
        copies = []
        for step in range(1, cols):
            slot = lax.rem(c + step, cols) * chans + h
            wait_block(buffer, sems, 0, slot)
            copy = pltpu.make_async_remote_copy(
                src_ref=buffer.at[0, slot], dst_ref=buffer.at[0, slot],
                send_sem=send_sems.at[base + blocks + cols - 1 + step],
                recv_sem=sems.at[0, slot],
                device_id=sibling, device_id_type=MESH,
            )
            copy.start()
            copies.append(copy)
        return copies

    def wait_column(buffer, sems, slot):
        @pl.when(off_diagonal)
        def _():
            wait_block(buffer, sems, 1, slot)

    started = send_block(raw, raw_sems, 0)
    w_copy = pltpu.make_async_remote_copy(
        src_ref=w_proj_ref, dst_ref=w_half, send_sem=w_sems.at[0], recv_sem=w_sems.at[1],
        device_id=sibling, device_id_type=MESH,
    )
    w_copy.start()

    ids = lax.broadcasted_iota(jnp.int32, (length, length), 0)
    lanes = lax.broadcasted_iota(jnp.int32, (length, length), 1)
    flags = jnp.where(ids == lanes, mask_ref[...].astype(jnp.float32), 0.0)
    mask_col[...] = jnp.broadcast_to(jnp.sum(flags, axis=-1, keepdims=True), (length, 2 * half))

    w_copy.wait()
    first_chan = h == 0
    for u in range(2):
        for w in range(4):
            mine = w_proj_ref[u, w].astype(jnp.float32)
            theirs = w_half[u, w].astype(jnp.float32)
            low = jnp.where(first_chan, mine, theirs)
            high = jnp.where(first_chan, theirs, mine)
            full = jnp.concatenate([low, high], axis=-1).astype(jnp.bfloat16)
            w_full[u, w // 2, :, (w % 2) * 2 * half:(w % 2 + 1) * 2 * half] = full

    lower = lax.broadcasted_iota(jnp.int32, (area, 2 * half), 1) < half

    def unpacked(which, pair_slot):
        even = raw[which, chans * pair_slot].astype(jnp.float32)
        odd = raw[which, chans * pair_slot + 1].astype(jnp.float32)
        first = jnp.where(lower, even, pltpu.roll(odd, half, 1))
        second = jnp.where(lower, pltpu.roll(even, half, 1), odd)
        return first, second

    def project(u, side, wide, outer_block, inner_block, keep):
        normed = normalize(
            wide, in_gain_ref[u:u + 1, :], in_bias_ref[u:u + 1, :]
        ).astype(jnp.bfloat16)
        if keep is not None:
            values[keep] = wide.astype(jnp.bfloat16)
            normed_own[keep] = normed
        both = jnp.dot(normed, w_full[u, side], preferred_element_type=jnp.float32)
        outer = mask_col[pl.ds(outer_block * edge, edge), :]
        inner = mask_col[pl.ds(inner_block * edge, edge), :]
        mask = outer[:, None, :] * inner[None, :, :]
        gated = sigmoid(both[:, 2 * half:]) * both[:, :2 * half]
        gated = gated.reshape(edge, edge, 2 * half) * mask
        return gated.astype(jnp.bfloat16).astype(jnp.float32)

    def mix(row_of):
        def step(k, totals):
            tile = tile_op[pl.ds(k * edge, edge), :]
            return tuple(
                totals[i] + spread_op[pl.ds(row_of(i, k), 1), :] * tile for i in range(edge)
            )
        zero = tuple(jnp.zeros((edge, 2 * half), jnp.float32) for _ in range(edge))
        totals = lax.fori_loop(0, length, step, zero, unroll=8)
        return jnp.concatenate(totals, axis=0)

    def finish(u, mixed, block):
        mixed = mixed.astype(jnp.bfloat16).astype(jnp.float32)
        mixed_norm = normalize(
            mixed, out_gain_ref[u:u + 1, :], out_bias_ref[u:u + 1, :]
        ).astype(jnp.bfloat16)
        projected = jnp.dot(mixed_norm, w_out_ref[u], preferred_element_type=jnp.float32)
        gate = sigmoid(jnp.dot(normed_own[block], w_gate_ref[u], preferred_element_type=jnp.float32))
        return (values[block].astype(jnp.float32) + gate * projected).astype(jnp.bfloat16)

    def right_blocks(step, carry):
        pair_slot = lax.rem(c + step, cols)
        wait_block(raw, raw_sems, 0, chans * pair_slot + 1 - h)
        for part, wide in enumerate(unpacked(0, pair_slot)):
            inner = chans * pair_slot + part
            gated = project(0, 1, wide, r, inner, None)
            for j in range(edge):
                tile_op[pl.ds(inner * area + j, edge, stride=edge), :] = gated[j]
        return carry

    right_blocks(0, 0)
    started += hand_on(raw, raw_sems, 0)
    lax.fori_loop(1, cols, right_blocks, 0)

    def left_blocks(pair_slot, carry):
        for part in range(chans):
            wait_column(raw, raw_sems, chans * pair_slot + part)
        for part, wide in enumerate(unpacked(away, pair_slot)):
            inner = chans * pair_slot + part
            gated = project(0, 0, wide, q, inner, inner)
            for i in range(edge):
                spread_op[pl.ds(i * length + inner * edge, edge), :] = gated[i]
        return carry

    lax.fori_loop(0, cols, left_blocks, 0)
    mid[0, q] = finish(0, mix(lambda i, k: i * length + k), r)

    started += send_block(mid, mid_sems, 2 * blocks)

    def left_columns(step, carry):
        pair_slot = lax.rem(c + step, cols)
        wait_block(mid, mid_sems, 0, chans * pair_slot + 1 - h)
        for part in range(chans):
            slot = chans * pair_slot + part
            gated = project(1, 0, mid[0, slot].astype(jnp.float32), slot, r, None)
            spread_op[pl.ds(slot * area, area), :] = gated.reshape(area, 2 * half)
        return carry

    left_columns(0, 0)
    started += hand_on(mid, mid_sems, 2 * blocks)
    lax.fori_loop(1, cols, left_columns, 0)

    def right_columns(slot, carry):
        wait_column(mid, mid_sems, slot)
        gated = project(1, 1, mid[away, slot].astype(jnp.float32), slot, q, slot)
        tile_op[pl.ds(slot * area, area), :] = gated.reshape(area, 2 * half)
        return carry

    lax.fori_loop(0, blocks, right_columns, 0)
    fin[h] = finish(1, mix(lambda i, k: k * edge + i), r)

    last = pltpu.make_async_remote_copy(
        src_ref=fin.at[h], dst_ref=fin.at[h], send_sem=fin_sems.at[0], recv_sem=fin_sems.at[1],
        device_id=sibling, device_id_type=MESH,
    )
    last.start()
    for copy in started:
        copy.wait_send()
    last.wait()
    for part in range(chans):
        block = fin[part].astype(jnp.float32)
        piece = jnp.where(first_chan, block[:, :half], block[:, half:])
        out_ref[:, part * edge:(part + 1) * edge, :] = (
            piece.reshape(edge, edge, half).astype(jnp.bfloat16)
        )


def local(sizes, pair, token_mask, w_proj, w_gate, w_out, in_gain, in_bias, out_gain, out_bias):
    rows, cols, chans = sizes
    edge, wide_cols, half = pair.shape
    blocks, area, length = rows, edge * edge, token_mask.shape[0]
    full = chans * half
    assert chans == 2 and rows == cols * chans and wide_cols == chans * edge
    vmem = pl.BlockSpec(memory_space=pltpu.VMEM)
    return pl.pallas_call(
        functools.partial(kernel, rows, cols, chans, edge),
        out_shape=jax.ShapeDtypeStruct(pair.shape, pair.dtype),
        in_specs=[vmem] * 9,
        out_specs=vmem,
        scratch_shapes=[
            pltpu.VMEM((2, blocks, area, full), jnp.bfloat16),
            pltpu.VMEM((2, blocks, area, full), jnp.bfloat16),
            pltpu.VMEM((chans, area, full), jnp.bfloat16),
            pltpu.VMEM(w_proj.shape, jnp.bfloat16),
            pltpu.VMEM((2, 2, full, 2 * full), jnp.bfloat16),
            pltpu.VMEM((length, full), jnp.float32),
            pltpu.VMEM((edge * length, full), jnp.float32),
            pltpu.VMEM((edge * length, full), jnp.float32),
            pltpu.VMEM((blocks, area, full), jnp.bfloat16),
            pltpu.VMEM((blocks, area, full), jnp.bfloat16),
            pltpu.SemaphoreType.DMA((4 * blocks,)),
            pltpu.SemaphoreType.DMA((2, blocks)),
            pltpu.SemaphoreType.DMA((2, blocks)),
            pltpu.SemaphoreType.DMA((2,)),
            pltpu.SemaphoreType.DMA((2,)),
        ],
        compiler_params=pltpu.CompilerParams(
            collective_id=0, has_side_effects=True, vmem_limit_bytes=48 * 1024 * 1024
        ),
    )(pair, token_mask.reshape(1, length), w_proj, w_gate, w_out, in_gain, in_bias, out_gain, out_bias)


def solution(mesh):
    sizes = tuple(mesh.shape[name] for name in ("row", "col", "chan"))
    return jax.shard_map(
        functools.partial(local, sizes),
        mesh=mesh,
        in_specs=(
            P(("groups", "row"), "col", "chan"),
            P("groups"),
            P(None, None, None, "chan"),
            P(),
            P(),
            P(),
            P(),
            P(),
            P(),
        ),
        out_specs=P(("groups", "row"), "col", "chan"),
        check_vma=False,
    )
```
